512 devices in a mesh: vocab: 128 (over y, z, core), width: 4 (over x).
Axes of the slice: x: 4, y: 4, z: 16, core: 2. Of those that a mesh axis runs over, the one named last changes fastest.
Arguments:
- hidden: bfloat16 [256, 4608], P(None, 'width'), may hold values from -6 to 6
- head_weight: bfloat16 [262144, 4608], P('vocab', 'width'), as said below
- targets: int32 [256], replicated, may hold values from 0 to 262143
- token_scale: float32 [256], replicated, may hold values from 8 to 64
Outputs:
- hidden_grad: bfloat16 [256, 4608], P('vocab', 'width')
The draws below stay inside these ranges and needn't reach their ends.
Inputs may be any that keep to these rules, and one draw needn't show every extreme that they name: Each row of head_weight is independent noise of its own scale.
All inputs are finite; a program needn't handle non-finite values.
Results may differ from the reference program's by a relative error of at most 0.0046.
Values may be sent and summed in bfloat16 or wider, within the bound.
No kernel may reach another device: no remote copies, remote signals or barrier semaphores. Data moves between devices by JAX's collectives and lax.ppermute only.
A program may use at most 64 MiB of HBM per device.

```python
import math
import jax
import jax.numpy as jnp

D = 4608
TOKENS = 256
VOCAB = 262144


def draw_head_weight(key, part):
    key = jax.random.fold_in(key, 7)
    scale_key, noise_key = jax.random.split(key)
    rows = jnp.arange(VOCAB, dtype=jnp.float32)
    rising = 1.0 + 0.25 * rows / VOCAB
    spread = 10.0 ** jax.random.uniform(scale_key, (VOCAB,), jnp.float32)
    row_sd = 0.4 * spread * rising / jnp.sqrt(jnp.float32(D))
    noise = jax.random.normal(noise_key, (VOCAB, D), jnp.float32)
    return (noise * row_sd[:, None]).astype(jnp.bfloat16)


def with_ends(values, rng, least, largest):
    dims = values.shape
    place = [jax.random.randint(jax.random.fold_in(rng, axis), (), 0, dims[axis]) for axis in range(len(dims))]
    values = values.at[tuple(place)].set(least)
    longest = dims.index(max(dims))
    place[longest] = (place[longest] + 1) % dims[longest]
    return values.at[tuple(place)].set(largest)


def shard_levels(own_key, dims, cuts, least, top_value):
    loudness, own = 1.0, jax.random.fold_in(own_key, 6)
    for dim, shards_of in cuts:
        heights = jnp.exp(jax.random.uniform(jax.random.fold_in(own, dim), (shards_of,), jnp.float32, least / len(cuts), top_value / len(cuts)))
        loudness = loudness * jnp.repeat(heights, dims[dim] // shards_of).reshape([-1 if axis == dim else 1 for axis in range(len(dims))])
    return loudness


def centred(rng, shape, scale, reach, cuts=(), held_as=jnp.bfloat16):
    entries = scale * jax.random.normal(rng, shape, jnp.float32)
    if cuts:
        entries = entries * shard_levels(rng, shape, cuts, -0.22, 0.18)
    return jnp.clip(entries, -reach, reach).astype(held_as)


def setup_inputs(seed: int = 0) -> dict:
    splits = jax.random.split(jax.random.key(seed), 5)
    hidden = centred(splits[0], (TOKENS, D), 1.0, 6.0, ((1, 4),))
    head_weight = draw_head_weight(jax.random.fold_in(splits[4], 71), 0)
    targets = with_ends(jax.random.randint(splits[2], (TOKENS,), 0, VOCAB), jax.random.fold_in(splits[2], 1), 0, VOCAB - 1).astype(jnp.int32)
    token_scale = jnp.clip(jnp.exp(jax.random.uniform(splits[3], (TOKENS,), jnp.float32, math.log(8.0), math.log(64.0))), 8.0, 64.0)
    return {"hidden": hidden, "head_weight": head_weight, "targets": targets, "token_scale": token_scale}


logit_cap = 30.0
zloss_weight = 0.001


def reference(hidden, head_weight, targets, token_scale):
    raw = jnp.dot(hidden, head_weight.T, preferred_element_type=jnp.float32)
    tangent = jnp.tanh(raw / logit_cap)
    capped = logit_cap * tangent
    exp_terms = jnp.exp(capped)
    total = jnp.sum(exp_terms, axis=1)
    log_total = jnp.log(total)
    weighting = token_scale * (1.0 + 2.0 * zloss_weight * log_total)
    matches = (targets[:, None] == jnp.arange(VOCAB, dtype=jnp.int32)[None, :]).astype(jnp.float32)
    capped_grad = weighting[:, None] * exp_terms / total[:, None] - token_scale[:, None] * matches
    raw_grad = (capped_grad * (1.0 - tangent * tangent)).astype(jnp.bfloat16)
    return jnp.dot(raw_grad, head_weight, preferred_element_type=jnp.float32).astype(jnp.bfloat16)
```

```python
import functools
import jax
import jax.numpy as jnp
from jax import lax
from jax.experimental import pallas as pl
from jax.experimental.pallas import tpu as pltpu
from jax.sharding import Mesh, PartitionSpec as P

logit_cap = 30.0
zloss_weight = 0.001

f32, bf16, i16, i32 = jnp.float32, jnp.bfloat16, jnp.int16, jnp.int32

SIDE = 16
LANES = 128
TOP = 32767.0


def exponent_of(largest):
    return jnp.floor(jnp.log2(jnp.maximum(largest, 1e-30))) - 14.0


def code(values, exponent):
    scaled = jnp.floor(values * jnp.exp2(-exponent) + 0.5)
    return jnp.clip(scaled, -TOP, TOP).astype(i32).astype(i16)


def to_f32(codes):
    return codes.astype(i32).astype(f32)


def token_order(sizes, tokens):
    ny, nz, nc = sizes
    pair = tokens // (ny * nz * nc)
    place = lax.broadcasted_iota(i32, (tokens, tokens), 0)
    token = lax.broadcasted_iota(i32, (tokens, tokens), 1)
    core = place // (ny * nz * pair)
    yz = (place // pair) % (ny * nz)
    r = place % pair
    return token == (yz * nc + core) * pair + r


def column_of(mask, row):
    return jnp.sum(jnp.where(mask, row, 0.0), axis=1, keepdims=True)


def eye(n):
    return lax.broadcasted_iota(i32, (n, n), 0) == lax.broadcasted_iota(i32, (n, n), 1)


def logits_kernel(sizes, hidden_ref, weight_ref, out_ref, ordered_ref):
    tokens = hidden_ref.shape[0]

    @pl.when(pl.program_id(0) == 0)
    def _():
        order = jnp.where(token_order(sizes, tokens), 1.0, 0.0).astype(bf16)
        ordered_ref[...] = jnp.dot(
            order, hidden_ref[...], preferred_element_type=f32
        ).astype(bf16)

    partial = lax.dot_general(
        ordered_ref[...], weight_ref[...], (((1,), (1,)), ((), ())), preferred_element_type=f32
    )
    exponent = exponent_of(jnp.max(jnp.abs(partial), axis=0, keepdims=True))
    out_ref[0, 0:tokens, :] = code(partial, exponent)
    out_ref[0, tokens:, :] = jnp.broadcast_to(
        exponent, (SIDE, exponent.shape[1])
    ).astype(i32).astype(i16)


def exp_kernel(sizes, codes_ref, targets_ref, out_ref):
    parts, rows, columns = codes_ref.shape
    tokens = rows - SIDE
    raw = None
    for part in range(parts):
        exponent = to_f32(codes_ref[part, tokens:, :])[0:1]
        term = to_f32(codes_ref[part, 0:tokens, :]) * jnp.exp2(exponent)
        raw = term if raw is None else raw + term
    tangent = jnp.tanh(raw / logit_cap)
    exp_terms = jnp.exp(logit_cap * tangent)
    slope = 1.0 - tangent * tangent
    grads = (exp_terms * slope).astype(bf16)
    sums = jnp.sum(exp_terms, axis=1, keepdims=True)
    targets = column_of(token_order(sizes, tokens), targets_ref[...].astype(f32))
    places = lax.broadcasted_iota(i32, raw.shape, 1).astype(f32)
    at_target = jnp.sum(jnp.where(targets == places, slope, 0.0), axis=1, keepdims=True)
    diagonal = eye(tokens)
    sum_row = jnp.sum(jnp.where(diagonal, sums, 0.0), axis=0, keepdims=True)
    target_row = jnp.sum(jnp.where(diagonal, at_target, 0.0), axis=0, keepdims=True)
    which = lax.broadcasted_iota(i32, (SIDE, tokens), 0)
    side = jnp.where(which == 0, sum_row, jnp.where(which == 1, target_row, 0.0))
    high = side.astype(bf16)
    low = (side - high.astype(f32)).astype(bf16)
    pieces = [high, low]
    if columns > 2 * tokens:
        pieces.append(jnp.zeros((SIDE, columns - 2 * tokens), bf16))
    side = jnp.concatenate(pieces, axis=1)
    for part in range(parts):
        out_ref[part, 0:tokens, :] = grads
        out_ref[part, tokens:, :] = side


def hidden_kernel(sizes, grads_ref, weight_ref, targets_ref, out_ref, side_ref):
    step = pl.program_id(0)
    nc = sizes[2]
    _, rows, columns = grads_ref.shape
    tokens = rows - SIDE
    width = weight_ref.shape[1]
    own = tokens // nc
    targets = column_of(token_order(sizes, tokens), targets_ref[...].astype(f32))
    places = (lax.broadcasted_iota(i32, (tokens, columns), 1) + step * columns).astype(f32)
    at_target = jnp.where(targets == places, 1.0, 0.0).astype(bf16)
    weight = weight_ref[...]
    soft = jnp.dot(grads_ref[0, 0:tokens, :], weight, preferred_element_type=f32)
    hard = jnp.dot(at_target, weight, preferred_element_type=f32)
    side = grads_ref[0, tokens:, :].astype(f32)
    side = side[:, 0:tokens] + side[:, tokens : 2 * tokens]

    @pl.when(step == 0)
    def _():
        side_ref[...] = side
        for c in range(nc):
            out_ref[c, :, 0:width] = soft[c * own : (c + 1) * own]
            out_ref[c, :, width : 2 * width] = hard[c * own : (c + 1) * own]

    @pl.when(step > 0)
    def _():
        side_ref[...] += side
        for c in range(nc):
            out_ref[c, :, 0:width] += soft[c * own : (c + 1) * own]
            out_ref[c, :, width : 2 * width] += hard[c * own : (c + 1) * own]

    @pl.when(step == pl.num_programs(0) - 1)
    def _():
        diagonal = eye(tokens)
        sums = column_of(diagonal, side_ref[0:1, :])
        slope = column_of(diagonal, side_ref[1:2, :])
        for c in range(nc):
            part = slice(c * own, (c + 1) * own)
            out_ref[c, :, width : 2 * width] *= slope[part]
            out_ref[c, :, 2 * width :] = jnp.broadcast_to(sums[part], (own, LANES))


def coded_rows(soft, hard, total):
    rows = soft.shape[0]
    soft_exp = exponent_of(jnp.max(jnp.abs(soft), axis=1, keepdims=True))
    hard_exp = exponent_of(jnp.max(jnp.abs(hard), axis=1, keepdims=True))
    total_exp = jnp.floor(jnp.log2(jnp.maximum(total, 1e-30))) - 24.0
    scaled = total * jnp.exp2(-total_exp)
    high = jnp.floor(scaled * (1.0 / 4096.0))
    low = scaled - high * 4096.0
    lane = lax.broadcasted_iota(i32, (rows, LANES), 1)
    side = jnp.where(lane == 0, soft_exp, 0.0)
    for at, value in enumerate((hard_exp, total_exp, high, low), 1):
        side = jnp.where(lane == at, value, side)
    side = side.astype(i32).astype(i16)
    return code(soft, soft_exp), code(hard, hard_exp), side


def decoded(codes, width):
    side = to_f32(codes[:, 2 * width :])
    soft = to_f32(codes[:, 0:width]) * jnp.exp2(side[:, 0:1])
    hard = to_f32(codes[:, width : 2 * width]) * jnp.exp2(side[:, 1:2])
    total = (side[:, 3:4] * 4096.0 + side[:, 4:5]) * jnp.exp2(side[:, 2:3])
    return soft, hard, total


def store_rows(out_ref, soft, hard, total, width):
    parts, rows, _ = out_ref.shape
    coded = coded_rows(soft, hard, total)
    at = 0
    for piece in coded:
        for part in range(parts):
            out_ref[part, :, at : at + piece.shape[1]] = piece[part * rows : (part + 1) * rows]
        at += piece.shape[1]


def cores_kernel(width, in_ref, out_ref):
    total = in_ref[0]
    for c in range(1, in_ref.shape[0]):
        total = total + in_ref[c]
    soft, hard = total[:, 0:width], total[:, width : 2 * width]
    store_rows(out_ref, soft, hard, total[:, 2 * width : 2 * width + 1], width)


def y_kernel(width, in_ref, out_ref):
    terms = [decoded(in_ref[part], width) for part in range(in_ref.shape[0])]
    soft, hard, total = (functools.reduce(jnp.add, t) for t in zip(*terms))
    store_rows(out_ref, soft, hard, total, width)


def whole(shape):
    return pl.BlockSpec(shape, lambda *_: (0,) * len(shape))


def params():
    return pltpu.CompilerParams(vmem_limit_bytes=40 * 1024 * 1024)


def on_device(sizes, hidden, head_weight, targets, token_scale):
    ny, nz, nc = sizes
    nw = lax.axis_size("w")
    tokens, width = hidden.shape
    vocab = head_weight.shape[0]
    columns = vocab // nw
    rows = tokens + SIDE
    pair = tokens // (ny * nz * nc)
    lanes = 2 * width + LANES
    device = (lax.axis_index("y") * nz + lax.axis_index("z")) * nc + lax.axis_index("c")
    shard_targets = (targets - device * vocab).reshape(1, tokens)
    block_targets = shard_targets - lax.axis_index("w") * columns

    codes = pl.pallas_call(
        functools.partial(logits_kernel, sizes),
        grid=(nw,),
        in_specs=[whole((tokens, width)), pl.BlockSpec((columns, width), lambda j: (j, 0))],
        out_specs=pl.BlockSpec((1, rows, columns), lambda j: (j, 0, 0)),
        out_shape=jax.ShapeDtypeStruct((nw, rows, columns), i16),
        scratch_shapes=[pltpu.VMEM((tokens, width), bf16)],
        compiler_params=params(),
        name="logits",
    )(hidden, head_weight)
    codes = lax.all_to_all(codes, "w", 0, 0, tiled=True)
    grads = pl.pallas_call(
        functools.partial(exp_kernel, sizes),
        out_shape=jax.ShapeDtypeStruct((nw, rows, columns), bf16),
        compiler_params=params(),
        name="exponentials",
    )(codes, block_targets)
    grads = lax.all_to_all(grads, "w", 0, 0, tiled=True)
    sums = pl.pallas_call(
        functools.partial(hidden_kernel, sizes),
        grid=(nw,),
        in_specs=[
            pl.BlockSpec((1, rows, columns), lambda j: (j, 0, 0)),
            pl.BlockSpec((columns, width), lambda j: (j, 0)),
            whole((1, tokens)),
        ],
        out_specs=whole((nc, tokens // nc, lanes)),
        out_shape=jax.ShapeDtypeStruct((nc, tokens // nc, lanes), f32),
        scratch_shapes=[pltpu.VMEM((SIDE, tokens), f32)],
        compiler_params=params(),
        name="hidden_partial",
    )(grads, head_weight, shard_targets)
    sums = lax.all_to_all(sums, "c", 0, 0, tiled=True)
    sums = pl.pallas_call(
        functools.partial(cores_kernel, width),
        out_shape=jax.ShapeDtypeStruct((ny, nz * pair, lanes), i16),
        compiler_params=params(),
        name="sum_cores",
    )(sums)
    sums = lax.all_to_all(sums, "y", 0, 0, tiled=True)
    sums = pl.pallas_call(
        functools.partial(y_kernel, width),
        out_shape=jax.ShapeDtypeStruct((1, nz * pair, lanes), i16),
        compiler_params=params(),
        name="sum_y",
    )(sums)
    sums = lax.all_to_all(sums.reshape(nz, pair, lanes), "z", 0, 0, tiled=True)
    soft, hard, total = decoded(sums.reshape(nz * pair, lanes), width)
    soft = jnp.sum(soft.reshape(nz, pair, width), axis=0)
    hard = jnp.sum(hard.reshape(nz, pair, width), axis=0)
    total = jnp.sum(total.reshape(nz, pair, 1), axis=0)
    scale = lax.dynamic_slice(token_scale, (device * pair,), (pair,))[:, None]
    weighting = scale * (1.0 + 2.0 * zloss_weight * jnp.log(total))
    return (weighting / total * soft - scale * hard).astype(bf16)


def solution(mesh):
    vocab, width = mesh.devices.shape
    sizes = (4, vocab // 8, 2)
    inner = Mesh(mesh.devices.reshape(*sizes, width), ("y", "z", "c", "w"))
    vocab_axes = ("y", "z", "c")
    placed = (P(None, "w"), P(vocab_axes, "w"), P(), P())
    return jax.shard_map(
        functools.partial(on_device, sizes),
        mesh=inner,
        in_specs=placed,
        out_specs=P(vocab_axes, "w"),
        check_vma=False,
    )
```

```python
import functools
import jax
import jax.numpy as jnp
from jax import lax
from jax.experimental import pallas as pl
from jax.experimental.pallas import tpu as pltpu
from jax.sharding import Mesh, PartitionSpec as P

logit_cap = 30.0
zloss_weight = 0.001

f32, bf16, i16, i32 = jnp.float32, jnp.bfloat16, jnp.int16, jnp.int32

SIDE = 16
LANES = 128
TOP = 32767.0
VMEM_BYTES = 20 * 1024 * 1024


def exponent_of(largest):
    return jnp.floor(jnp.log2(jnp.maximum(largest, 1e-30))) - 14.0


def code(values, exponent):
    scaled = jnp.floor(values * jnp.exp2(-exponent) + 0.5)
    return jnp.clip(scaled, -TOP, TOP).astype(i32).astype(i16)


def to_f32(codes):
    return codes.astype(i32).astype(f32)


def token_order(sizes, tokens):
    ny, nz, nc = sizes
    pair = tokens // (ny * nz * nc)
    place = lax.broadcasted_iota(i32, (tokens, tokens), 0)
    token = lax.broadcasted_iota(i32, (tokens, tokens), 1)
    core = place // (ny * nz * pair)
    yz = (place // pair) % (ny * nz)
    r = place % pair
    return token == (yz * nc + core) * pair + r


def column_of(mask, row):
    return jnp.sum(jnp.where(mask, row, 0.0), axis=1, keepdims=True)


def eye(n):
    return lax.broadcasted_iota(i32, (n, n), 0) == lax.broadcasted_iota(i32, (n, n), 1)


def rows_of(part, columns):
    return pl.ds(pl.multiple_of(part * columns, columns), columns)


def coded_logits(ordered, weight, out_ref):
    tokens = ordered.shape[0]
    partial = raw_part(ordered, weight)
    exponent = exponent_of(jnp.max(jnp.abs(partial), axis=0, keepdims=True))
    out_ref[0:tokens, :] = code(partial, exponent)
    out_ref[tokens:, :] = jnp.broadcast_to(
        exponent, (SIDE, exponent.shape[1])
    ).astype(i32).astype(i16)


def raw_part(ordered, weight):
    return lax.dot_general(ordered, weight, (((1,), (1,)), ((), ())), preferred_element_type=f32)


def far_logits_kernel(
    sizes, parts, hidden_hbm, weight_hbm, targets_hbm, scale_hbm,
    out_ref, ordered_ref, place_ref, own_scale_ref,
    hidden_ref, weight_ref, targets_ref, scale_ref, sems,
):
    tokens = hidden_ref.shape[0]
    pair = own_scale_ref.shape[0]
    columns = out_ref.shape[1]
    far = lax.rem(lax.axis_index("w") + parts // 2, parts)
    copies = [
        pltpu.make_async_copy(source, target, sems.at[at])
        for at, (source, target) in enumerate(
            (
                (hidden_hbm, hidden_ref),
                (targets_hbm, targets_ref),
                (scale_hbm, scale_ref),
                (weight_hbm.at[rows_of(far, columns)], weight_ref),
            )
        )
    ]
    for copy in copies:
        copy.start()
    ordering = token_order(sizes, tokens)
    order = jnp.where(ordering, 1.0, 0.0).astype(bf16)
    ny, nz, nc = sizes
    device = (lax.axis_index("y") * nz + lax.axis_index("z")) * nc + lax.axis_index("c")
    copies[0].wait()
    ordered = jnp.dot(order, hidden_ref[...], preferred_element_type=f32).astype(bf16)
    ordered_ref[...] = ordered
    copies[1].wait()
    place = column_of(ordering, (targets_ref[...] - device * (parts * columns)).astype(f32))
    place_ref[...] = jnp.broadcast_to(place, place_ref.shape)
    copies[2].wait()
    mine = lax.broadcasted_iota(i32, (pair, tokens), 1) == (
        device * pair + lax.broadcasted_iota(i32, (pair, tokens), 0)
    )
    own_scale_ref[...] = jnp.broadcast_to(column_of(mine, scale_ref[...]), own_scale_ref.shape)
    copies[3].wait()
    coded_logits(ordered, weight_ref[...], out_ref)


def near_logits_kernel(
    parts, steps, ordered_ref, weight_hbm, *refs
):
    out_refs, own_ref, weight_ref, sems = refs[: len(steps)], refs[-3], refs[-2], refs[-1]
    columns = own_ref.shape[1]
    me = lax.axis_index("w")
    copies = [
        pltpu.make_async_copy(
            weight_hbm.at[rows_of(lax.rem(me + step, parts), columns)],
            weight_ref.at[at],
            sems.at[at],
        )
        for at, step in enumerate((*steps, 0))
    ]
    for copy in copies:
        copy.start()
    ordered = ordered_ref[...]
    for at, out_ref in enumerate(out_refs):
        copies[at].wait()
        coded_logits(ordered, weight_ref[at], out_ref)
    copies[-1].wait()
    own_ref[...] = raw_part(ordered, weight_ref[len(steps)])


def exp_kernel(own_ref, *refs):
    codes_refs, place_ref, out_ref = refs[:-2], refs[-2], refs[-1]
    tokens, columns = own_ref.shape
    raw = own_ref[...]
    for codes_ref in codes_refs:
        exponent = to_f32(codes_ref[tokens:, :])[0:1]
        raw = raw + to_f32(codes_ref[0:tokens, :]) * jnp.exp2(exponent)
    tangent = jnp.tanh(raw / logit_cap)
    exp_terms = jnp.exp(logit_cap * tangent)
    slope = 1.0 - tangent * tangent
    sums = jnp.sum(exp_terms, axis=1, keepdims=True)
    targets = place_ref[:, 0:1]
    places = lax.broadcasted_iota(i32, raw.shape, 1) + lax.axis_index("w") * columns
    at_target = jnp.sum(
        jnp.where(targets == places.astype(f32), slope, 0.0), axis=1, keepdims=True
    )
    diagonal = eye(tokens)
    sum_row = jnp.sum(jnp.where(diagonal, sums, 0.0), axis=0, keepdims=True)
    target_row = jnp.sum(jnp.where(diagonal, at_target, 0.0), axis=0, keepdims=True)
    which = lax.broadcasted_iota(i32, (SIDE, tokens), 0)
    side = jnp.where(which == 0, sum_row, jnp.where(which == 1, target_row, 0.0))
    high = side.astype(bf16)
    low = (side - high.astype(f32)).astype(bf16)
    pieces = [high, low]
    if columns > 2 * tokens:
        pieces.append(jnp.zeros((SIDE, columns - 2 * tokens), bf16))
    out_ref[0:tokens, :] = (exp_terms * slope).astype(bf16)
    out_ref[tokens:, :] = jnp.concatenate(pieces, axis=1)


def side_of(grads_ref, tokens):
    side = grads_ref[tokens:, :].astype(f32)
    return side[:, 0:tokens] + side[:, tokens : 2 * tokens]


def own_hidden_kernel(
    parts, grads_ref, weight_hbm, place_ref, soft_ref, hard_ref, side_ref, weight_ref, sems
):
    tokens, _ = soft_ref.shape
    columns = grads_ref.shape[1]
    me = lax.axis_index("w")
    order = [lax.rem(me + step, parts) for step in range(parts)]
    copies = [
        pltpu.make_async_copy(
            weight_hbm.at[rows_of(part, columns)], weight_ref.at[rows_of(part, columns)], sems.at[at]
        )
        for at, part in enumerate(order)
    ]
    for copy in copies:
        copy.start()
    targets = place_ref[:, 0:1]
    lane = lax.broadcasted_iota(i32, (tokens, columns), 1)
    side_ref[...] = side_of(grads_ref, tokens)
    hard = None
    for at, part in enumerate(order):
        at_target = targets == (lane + part * columns).astype(f32)
        at_target = jnp.where(at_target, 1.0, 0.0).astype(bf16)
        copies[at].wait()
        weight = weight_ref[rows_of(part, columns)]
        if at == 0:
            soft_ref[...] = jnp.dot(
                grads_ref[0:tokens, :], weight, preferred_element_type=f32
            )
        term = jnp.dot(at_target, weight, preferred_element_type=f32)
        hard = term if hard is None else hard + term
    hard_ref[...] = hard


def near_hidden_kernel(parts, steps, soft_ref, side_ref, weight_ref, *refs):
    grads_refs, out_ref, out_side_ref = refs[:-2], refs[-2], refs[-1]
    tokens = soft_ref.shape[0]
    me = lax.axis_index("w")
    soft, side = soft_ref[...], side_ref[...]
    for step, grads_ref in zip(steps, grads_refs, strict=True):
        columns = grads_ref.shape[1]
        weight = weight_ref[rows_of(lax.rem(me + parts - step, parts), columns)]
        soft = soft + jnp.dot(grads_ref[0:tokens, :], weight, preferred_element_type=f32)
        side = side + side_of(grads_ref, tokens)
    out_ref[...] = soft
    out_side_ref[...] = side


def far_hidden_kernel(
    parts, soft_ref, side_ref, weight_ref, hard_ref, grads_ref, mine_ref, other_ref, sum_ref
):
    tokens, width = soft_ref.shape
    own = mine_ref.shape[0]
    columns = grads_ref.shape[1]
    far = lax.rem(lax.axis_index("w") + parts // 2, parts)
    weight = weight_ref[rows_of(far, columns)]
    soft = soft_ref[...] + jnp.dot(
        grads_ref[0:tokens, :], weight, preferred_element_type=f32
    )
    side = side_ref[...] + side_of(grads_ref, tokens)
    diagonal = eye(tokens)
    sums = column_of(diagonal, side[0:1, :])
    slope = column_of(diagonal, side[1:2, :])
    sum_ref[:, 0:width] = soft
    sum_ref[:, width : 2 * width] = hard_ref[...] * slope
    sum_ref[:, 2 * width :] = jnp.broadcast_to(sums, (tokens, LANES))
    core = lax.axis_index("c")
    mine_ref[...] = sum_ref[rows_of(core, own)]
    other_ref[...] = sum_ref[rows_of(1 - core, own)]


def coded_rows(soft, hard, total):
    rows = soft.shape[0]
    soft_exp = exponent_of(jnp.max(jnp.abs(soft), axis=1, keepdims=True))
    hard_exp = exponent_of(jnp.max(jnp.abs(hard), axis=1, keepdims=True))
    total_exp = jnp.floor(jnp.log2(jnp.maximum(total, 1e-30))) - 24.0
    scaled = total * jnp.exp2(-total_exp)
    high = jnp.floor(scaled * (1.0 / 4096.0))
    low = scaled - high * 4096.0
    lane = lax.broadcasted_iota(i32, (rows, LANES), 1)
    side = jnp.where(lane == 0, soft_exp, 0.0)
    for at, value in enumerate((hard_exp, total_exp, high, low), 1):
        side = jnp.where(lane == at, value, side)
    side = side.astype(i32).astype(i16)
    return code(soft, soft_exp), code(hard, hard_exp), side


def decoded(codes, width):
    side = to_f32(codes[:, 2 * width :])
    soft = to_f32(codes[:, 0:width]) * jnp.exp2(side[:, 0:1])
    hard = to_f32(codes[:, width : 2 * width]) * jnp.exp2(side[:, 1:2])
    total = (side[:, 3:4] * 4096.0 + side[:, 4:5]) * jnp.exp2(side[:, 2:3])
    return soft, hard, total


def store_rows(out_ref, soft, hard, total, width):
    parts, rows, _ = out_ref.shape
    coded = coded_rows(soft, hard, total)
    at = 0
    for piece in coded:
        for part in range(parts):
            out_ref[part, :, at : at + piece.shape[1]] = piece[part * rows : (part + 1) * rows]
        at += piece.shape[1]


def cores_kernel(width, mine_ref, other_ref, out_ref):
    total = mine_ref[...] + other_ref[...]
    soft, hard = total[:, 0:width], total[:, width : 2 * width]
    store_rows(out_ref, soft, hard, total[:, 2 * width : 2 * width + 1], width)


def y_kernel(width, in_ref, out_ref):
    terms = [decoded(in_ref[part], width) for part in range(in_ref.shape[0])]
    soft, hard, total = (functools.reduce(jnp.add, t) for t in zip(*terms))
    store_rows(out_ref, soft, hard, total, width)


def z_kernel(width, in_ref, scale_ref, out_ref):
    terms = [decoded(in_ref[part], width) for part in range(in_ref.shape[0])]
    soft, hard, total = (functools.reduce(jnp.add, t) for t in zip(*terms))
    scale = scale_ref[:, 0:1]
    weighting = scale * (1.0 + 2.0 * zloss_weight * jnp.log(total))
    out_ref[...] = (weighting / total * soft - scale * hard).astype(bf16)


def params():
    return pltpu.CompilerParams(vmem_limit_bytes=VMEM_BYTES)


def on_device(sizes, hidden, head_weight, targets, token_scale):
    ny, nz, nc = sizes
    nw = lax.axis_size("w")
    tokens, width = hidden.shape
    vocab = head_weight.shape[0]
    columns = vocab // nw
    rows = tokens + SIDE
    pair = tokens // (ny * nz * nc)
    lanes = 2 * width + LANES
    hbm = pl.BlockSpec(memory_space=pltpu.HBM)
    vmem = pl.BlockSpec(memory_space=pltpu.VMEM)
    steps = tuple(k for k in range(1, nw) if k != nw // 2)

    def shape(*dims, dtype=f32):
        return jax.ShapeDtypeStruct(dims, dtype)

    def send(x, step):
        return lax.ppermute(x, "w", [(i, (i + step) % nw) for i in range(nw)])

    in_hbm = functools.partial(pltpu.with_memory_space_constraint, memory_space=pltpu.HBM)
    weight_hbm = in_hbm(head_weight)
    far, ordered, place, scale = pl.pallas_call(
        functools.partial(far_logits_kernel, sizes, nw),
        in_specs=[hbm] * 4,
        out_specs=[vmem] * 4,
        out_shape=[
            shape(rows, columns, dtype=i16),
            shape(tokens, width, dtype=bf16),
            shape(tokens, LANES),
            shape(pair, LANES),
        ],
        scratch_shapes=[
            pltpu.VMEM((tokens, width), bf16),
            pltpu.VMEM((columns, width), bf16),
            pltpu.VMEM((1, tokens), i32),
            pltpu.VMEM((1, tokens), f32),
            pltpu.SemaphoreType.DMA((4,)),
        ],
        compiler_params=params(),
        name="far_logits",
    )(
        in_hbm(hidden),
        weight_hbm,
        in_hbm(targets.reshape(1, tokens)),
        in_hbm(token_scale.reshape(1, tokens)),
    )
    far = send(far, nw // 2)
    *near, own = pl.pallas_call(
        functools.partial(near_logits_kernel, nw, steps),
        in_specs=[vmem, hbm],
        out_specs=[vmem] * (len(steps) + 1),
        out_shape=[shape(rows, columns, dtype=i16)] * len(steps) + [shape(tokens, columns)],
        scratch_shapes=[
            pltpu.VMEM((len(steps) + 1, columns, width), bf16),
            pltpu.SemaphoreType.DMA((len(steps) + 1,)),
        ],
        compiler_params=params(),
        name="near_logits",
    )(ordered, weight_hbm)
    near = [send(x, step) for x, step in zip(near, steps, strict=True)]
    grads = pl.pallas_call(
        exp_kernel,
        out_shape=shape(rows, columns, dtype=bf16),
        compiler_params=params(),
        name="exponentials",
    )(own, far, *near, place)
    far = send(grads, nw // 2)
    near = [send(grads, step) for step in steps]
    soft, hard, side, weight = pl.pallas_call(
        functools.partial(own_hidden_kernel, nw),
        in_specs=[vmem, hbm, vmem],
        out_specs=[vmem] * 4,
        out_shape=[
            shape(tokens, width),
            shape(tokens, width),
            shape(SIDE, tokens),
            shape(vocab, width, dtype=bf16),
        ],
        scratch_shapes=[pltpu.SemaphoreType.DMA((nw,))],
        compiler_params=params(),
        name="own_hidden",
    )(grads, weight_hbm, place)
    soft, side = pl.pallas_call(
        functools.partial(near_hidden_kernel, nw, steps),
        out_shape=[shape(tokens, width), shape(SIDE, tokens)],
        compiler_params=params(),
        name="near_hidden",
    )(soft, side, weight, *near)
    mine, other = pl.pallas_call(
        functools.partial(far_hidden_kernel, nw),
        out_shape=[shape(tokens // nc, lanes)] * 2,
        scratch_shapes=[pltpu.VMEM((tokens, lanes), f32)],
        compiler_params=params(),
        name="far_hidden",
    )(soft, side, weight, hard, far)
    other = lax.ppermute(other, "c", [(0, 1), (1, 0)])
    sums = pl.pallas_call(
        functools.partial(cores_kernel, width),
        out_shape=jax.ShapeDtypeStruct((ny, nz * pair, lanes), i16),
        compiler_params=params(),
        name="sum_cores",
    )(mine, other)
    sums = lax.all_to_all(sums, "y", 0, 0, tiled=True)
    sums = pl.pallas_call(
        functools.partial(y_kernel, width),
        out_shape=jax.ShapeDtypeStruct((nz, pair, lanes), i16),
        compiler_params=params(),
        name="sum_y",
    )(sums)
    sums = lax.all_to_all(sums, "z", 0, 0, tiled=True)
    return pl.pallas_call(
        functools.partial(z_kernel, width),
        out_shape=jax.ShapeDtypeStruct((pair, width), bf16),
        compiler_params=params(),
        name="sum_z",
    )(sums, scale)


def solution(mesh):
    vocab, width = mesh.devices.shape
    sizes = (4, vocab // 8, 2)
    inner = Mesh(mesh.devices.reshape(*sizes, width), ("y", "z", "c", "w"))
    vocab_axes = ("y", "z", "c")
    placed = (P(None, "w"), P(vocab_axes, "w"), P(), P())
    return jax.shard_map(
        functools.partial(on_device, sizes),
        mesh=inner,
        in_specs=placed,
        out_specs=P(vocab_axes, "w"),
        check_vma=False,
    )
```

```python
import functools
import jax
import jax.numpy as jnp
from jax import lax
from jax.experimental import pallas as pl
from jax.experimental.pallas import tpu as pltpu
from jax.sharding import Mesh, PartitionSpec as P

logit_cap = 30.0
zloss_weight = 0.001

f32, bf16, i16, i32 = jnp.float32, jnp.bfloat16, jnp.int16, jnp.int32

SIDE = 16
LANES = 128
TOP = 32767.0
VMEM_BYTES = 18 * 1024 * 1024


def exponent_of(largest):
    return jnp.floor(jnp.log2(jnp.maximum(largest, 1e-30))) - 14.0


def code(values, exponent):
    scaled = jnp.floor(values * jnp.exp2(-exponent) + 0.5)
    return jnp.clip(scaled, -TOP, TOP).astype(i32).astype(i16)


def to_f32(codes):
    return codes.astype(i32).astype(f32)


def token_order(sizes, tokens):
    ny, nz, nc = sizes
    pair = tokens // (ny * nz * nc)
    place = lax.broadcasted_iota(i32, (tokens, tokens), 0)
    token = lax.broadcasted_iota(i32, (tokens, tokens), 1)
    core = place // (ny * nz * pair)
    yz = (place // pair) % (ny * nz)
    r = place % pair
    return token == (yz * nc + core) * pair + r


def column_of(mask, row):
    return jnp.sum(jnp.where(mask, row, 0.0), axis=1, keepdims=True)


def eye(n):
    return lax.broadcasted_iota(i32, (n, n), 0) == lax.broadcasted_iota(i32, (n, n), 1)


def rows_of(part, columns):
    return pl.ds(pl.multiple_of(part * columns, columns), columns)


def coded_logits(ordered, weight, out_ref):
    tokens = ordered.shape[0]
    partial = lax.dot_general(
        ordered, weight, (((1,), (1,)), ((), ())), preferred_element_type=f32
    )
    exponent = exponent_of(jnp.max(jnp.abs(partial), axis=0, keepdims=True))
    out_ref[0:tokens, :] = code(partial, exponent)
    out_ref[tokens:, :] = jnp.broadcast_to(
        exponent, (SIDE, exponent.shape[1])
    ).astype(i32).astype(i16)


def logits_kernel(
    sizes, hidden_hbm, weight_hbm, targets_hbm, scale_hbm,
    out_ref, place_ref, own_scale_ref, hard_ref, weight_ref,
    hidden_ref, part_ref, targets_ref, scale_ref, sems, weight_sems,
):
    tokens = hidden_ref.shape[0]
    pair = own_scale_ref.shape[0]
    parts, _, columns = out_ref.shape
    sources = [(hidden_hbm, hidden_ref), (targets_hbm, targets_ref), (scale_hbm, scale_ref)]
    for part in range(parts):
        sources.append((weight_hbm.at[pl.ds(part * columns, columns)], part_ref.at[part]))
    copies = [
        pltpu.make_async_copy(source, target, sems.at[at])
        for at, (source, target) in enumerate(sources)
    ]
    for copy in copies:
        copy.start()
    ordering = token_order(sizes, tokens)
    order = jnp.where(ordering, 1.0, 0.0).astype(bf16)
    ny, nz, nc = sizes
    device = (lax.axis_index("y") * nz + lax.axis_index("z")) * nc + lax.axis_index("c")
    for copy in copies[0:3]:
        copy.wait()
    ordered = jnp.dot(order, hidden_ref[...], preferred_element_type=f32).astype(bf16)
    place = column_of(ordering, (targets_ref[...] - device * (parts * columns)).astype(f32))
    place_ref[...] = jnp.broadcast_to(place, place_ref.shape)
    mine = lax.broadcasted_iota(i32, (pair, tokens), 1) == (
        device * pair + lax.broadcasted_iota(i32, (pair, tokens), 0)
    )
    own_scale_ref[...] = jnp.broadcast_to(column_of(mine, scale_ref[...]), own_scale_ref.shape)
    for part in range(parts):
        copies[3 + part].wait()
        coded_logits(ordered, part_ref[part], out_ref.at[part])

    @pl.when(lax.axis_index("c") == 0)
    def _():
        target_rows(weight_hbm, place_ref, hard_ref, weight_ref, weight_sems)


def exp_kernel(codes_ref, place_ref, out_ref):
    parts, rows, columns = codes_ref.shape
    tokens = rows - SIDE
    raw = None
    for part in range(parts):
        exponent = to_f32(codes_ref[part, tokens:, :])[0:1]
        term = to_f32(codes_ref[part, 0:tokens, :]) * jnp.exp2(exponent)
        raw = term if raw is None else raw + term
    tangent = jnp.tanh(raw / logit_cap)
    exp_terms = jnp.exp(logit_cap * tangent)
    slope = 1.0 - tangent * tangent
    sums = jnp.sum(exp_terms, axis=1, keepdims=True)
    targets = place_ref[:, 0:1]
    places = lax.broadcasted_iota(i32, raw.shape, 1) + lax.axis_index("w") * columns
    at_target = jnp.sum(
        jnp.where(targets == places.astype(f32), slope, 0.0), axis=1, keepdims=True
    )
    diagonal = eye(tokens)
    sum_row = jnp.sum(jnp.where(diagonal, sums, 0.0), axis=0, keepdims=True)
    target_row = jnp.sum(jnp.where(diagonal, at_target, 0.0), axis=0, keepdims=True)
    which = lax.broadcasted_iota(i32, (SIDE, tokens), 0)
    side = jnp.where(which == 0, sum_row, jnp.where(which == 1, target_row, 0.0))
    high = side.astype(bf16)
    low = (side - high.astype(f32)).astype(bf16)
    pieces = [high, low]
    if columns > 2 * tokens:
        pieces.append(jnp.zeros((SIDE, columns - 2 * tokens), bf16))
    grads = (exp_terms * slope).astype(bf16)
    side = jnp.concatenate(pieces, axis=1)
    for part in range(out_ref.shape[0]):
        out_ref[part, 0:tokens, :] = grads
        out_ref[part, tokens:, :] = side


def target_rows(weight_hbm, place_ref, rows_ref, weight_ref, sems):
    tokens = rows_ref.shape[0]
    blocks = sems.shape[0]
    columns = weight_ref.shape[0] // blocks
    copies = []
    for at in range(blocks):
        block = pl.ds(at * columns, columns)
        copies.append(
            pltpu.make_async_copy(weight_hbm.at[block], weight_ref.at[block], sems.at[at])
        )
        copies[-1].start()
    targets = place_ref[:, 0:1]
    lane = lax.broadcasted_iota(i32, (tokens, columns), 1)
    total = None
    for at in range(blocks):
        at_target = targets == (lane + at * columns).astype(f32)
        at_target = jnp.where(at_target, 1.0, 0.0).astype(bf16)
        copies[at].wait()
        weight = weight_ref[pl.ds(at * columns, columns)]
        term = jnp.dot(at_target, weight, preferred_element_type=f32)
        total = term if total is None else total + term
    rows_ref[...] = total.astype(bf16)


def hidden_kernel(
    grads_ref, weight_hbm, place_ref, hard_ref, weight_ref, mine_ref, other_ref,
    late_hard_ref, late_weight_ref, sum_ref, sems,
):
    @pl.when(lax.axis_index("c") == 0)
    def _():
        hidden_work(grads_ref, weight_ref, hard_ref, mine_ref, other_ref, sum_ref)

    @pl.when(lax.axis_index("c") == 1)
    def _():
        target_rows(weight_hbm, place_ref, late_hard_ref, late_weight_ref, sems)
        hidden_work(grads_ref, late_weight_ref, late_hard_ref, mine_ref, other_ref, sum_ref)


def hidden_work(grads_ref, weight_ref, hard_ref, mine_ref, other_ref, sum_ref):
    parts, rows, columns = grads_ref.shape
    tokens, width = rows - SIDE, weight_ref.shape[1]
    own = mine_ref.shape[0]
    side = None
    for part in range(parts):
        term = grads_ref[part, tokens:, :].astype(f32)
        term = term[:, 0:tokens] + term[:, tokens : 2 * tokens]
        side = term if side is None else side + term
    diagonal = eye(tokens)
    sums = column_of(diagonal, side[0:1, :])
    slope = column_of(diagonal, side[1:2, :])
    sum_ref[:, width : 2 * width] = hard_ref[...].astype(f32) * slope
    sum_ref[:, 2 * width :] = jnp.broadcast_to(sums, (tokens, LANES))
    soft = None
    for part in range(parts):
        weight = weight_ref[pl.ds(part * columns, columns)]
        term = jnp.dot(grads_ref[part, 0:tokens, :], weight, preferred_element_type=f32)
        soft = term if soft is None else soft + term
    sum_ref[:, 0:width] = soft
    core = lax.axis_index("c")
    mine_ref[...] = sum_ref[rows_of(core, own)]
    theirs = sum_ref[rows_of(1 - core, own)]
    store_rows(other_ref, theirs[:, 0:width], theirs[:, width : 2 * width], theirs[:, 2 * width : 2 * width + 1])


def scalar_codes(values):
    exponent = jnp.floor(jnp.log2(jnp.maximum(values, 1e-30))) - 24.0
    scaled = values * jnp.exp2(-exponent)
    high = jnp.floor(scaled * (1.0 / 4096.0))
    return [exponent, high, scaled - high * 4096.0]


def scalar_of(side, at):
    return (side[:, at + 1 : at + 2] * 4096.0 + side[:, at + 2 : at + 3]) * jnp.exp2(
        side[:, at : at + 1]
    )


def in_lanes(columns):
    lane = lax.broadcasted_iota(i32, (columns[0].shape[0], LANES), 1)
    side = jnp.zeros(lane.shape, f32)
    for at, value in enumerate(columns):
        side = jnp.where(lane == at, value, side)
    return side.astype(i32).astype(i16)


def row_exponent(values):
    return exponent_of(jnp.max(jnp.abs(values), axis=1, keepdims=True))


def store_rows(out_ref, soft, hard, total):
    soft_exp, hard_exp = row_exponent(soft), row_exponent(hard)
    pieces = (
        code(soft, soft_exp),
        code(hard, hard_exp),
        in_lanes([soft_exp, hard_exp, *scalar_codes(total)]),
    )
    parts, rows, _ = out_ref.shape
    at = 0
    for piece in pieces:
        for part in range(parts):
            out_ref[part, :, at : at + piece.shape[1]] = piece[part * rows : (part + 1) * rows]
        at += piece.shape[1]


def decoded_sum(width, in_ref):
    sums = None
    for part in range(in_ref.shape[0]):
        side = to_f32(in_ref[part, :, 2 * width :])
        terms = (
            to_f32(in_ref[part, :, 0:width]) * jnp.exp2(side[:, 0:1]),
            to_f32(in_ref[part, :, width : 2 * width]) * jnp.exp2(side[:, 1:2]),
            scalar_of(side, 2),
        )
        sums = terms if sums is None else tuple(a + b for a, b in zip(sums, terms))
    return sums


def cores_kernel(width, mine_ref, other_ref, out_ref):
    soft, hard, total = decoded_sum(width, other_ref)
    soft = soft + mine_ref[:, 0:width]
    hard = hard + mine_ref[:, width : 2 * width]
    store_rows(out_ref, soft, hard, total + mine_ref[:, 2 * width : 2 * width + 1])


def y_kernel(width, in_ref, out_ref):
    store_rows(out_ref, *decoded_sum(width, in_ref))


def z_kernel(width, in_ref, scale_ref, out_ref):
    soft, hard, total = decoded_sum(width, in_ref)
    scale = scale_ref[:, 0:1]
    weighting = scale * (1.0 + 2.0 * zloss_weight * jnp.log(total))
    out_ref[...] = (weighting / total * soft - scale * hard).astype(bf16)


def params():
    return pltpu.CompilerParams(vmem_limit_bytes=VMEM_BYTES)


def on_device(sizes, hidden, head_weight, targets, token_scale):
    ny, nz, nc = sizes
    nw = lax.axis_size("w")
    tokens, width = hidden.shape
    vocab = head_weight.shape[0]
    columns = vocab // nw
    rows = tokens + SIDE
    pair = tokens // (ny * nz * nc)
    lanes = 2 * width + LANES
    hbm = pl.BlockSpec(memory_space=pltpu.HBM)
    vmem = pl.BlockSpec(memory_space=pltpu.VMEM)

    def shape(*dims, dtype=f32):
        return jax.ShapeDtypeStruct(dims, dtype)

    def swap(x):
        return lax.ppermute(x, "c", [(0, 1), (1, 0)])

    in_hbm = functools.partial(pltpu.with_memory_space_constraint, memory_space=pltpu.HBM)
    weight_hbm = in_hbm(head_weight)
    hard_shapes = [shape(tokens, width, dtype=bf16), shape(vocab, width, dtype=bf16)]
    codes, place, scale, *hard = pl.pallas_call(
        functools.partial(logits_kernel, sizes),
        in_specs=[hbm] * 4,
        out_specs=[vmem] * 5,
        out_shape=[
            shape(nw, rows, columns, dtype=i16),
            shape(tokens, LANES),
            shape(pair, LANES),
            *hard_shapes,
        ],
        scratch_shapes=[
            pltpu.VMEM((tokens, width), bf16),
            pltpu.VMEM((nw, columns, width), bf16),
            pltpu.VMEM((1, tokens), i32),
            pltpu.VMEM((1, tokens), f32),
            pltpu.SemaphoreType.DMA((nw + 3,)),
            pltpu.SemaphoreType.DMA((nw,)),
        ],
        compiler_params=params(),
        name="logits",
    )(
        in_hbm(hidden),
        weight_hbm,
        in_hbm(targets.reshape(1, tokens)),
        in_hbm(token_scale.reshape(1, tokens)),
    )
    codes = lax.all_to_all(codes, "w", 0, 0, tiled=True)
    grads = pl.pallas_call(
        exp_kernel,
        out_shape=shape(nw, rows, columns, dtype=bf16),
        compiler_params=params(),
        name="exponentials",
    )(codes, place)
    grads = lax.all_to_all(grads, "w", 0, 0, tiled=True)
    mine, other = pl.pallas_call(
        hidden_kernel,
        in_specs=[vmem, hbm] + [vmem] * 3,
        out_specs=[vmem] * 2,
        out_shape=[shape(tokens // nc, lanes), shape(1, tokens // nc, lanes, dtype=i16)],
        scratch_shapes=[
            pltpu.VMEM((tokens, width), bf16),
            pltpu.VMEM((vocab, width), bf16),
            pltpu.VMEM((tokens, lanes), f32),
            pltpu.SemaphoreType.DMA((nw,)),
        ],
        compiler_params=params(),
        name="hidden_partial",
    )(grads, weight_hbm, place, *hard)
    other = swap(other)
    sums = pl.pallas_call(
        functools.partial(cores_kernel, width),
        out_shape=shape(ny, nz * pair, lanes, dtype=i16),
        compiler_params=params(),
        name="sum_cores",
    )(mine, other)
    sums = lax.all_to_all(sums, "y", 0, 0, tiled=True)
    sums = pl.pallas_call(
        functools.partial(y_kernel, width),
        out_shape=shape(nz, pair, lanes, dtype=i16),
        compiler_params=params(),
        name="sum_y",
    )(sums)
    sums = lax.all_to_all(sums, "z", 0, 0, tiled=True)
    return pl.pallas_call(
        functools.partial(z_kernel, width),
        out_shape=shape(pair, width, dtype=bf16),
        compiler_params=params(),
        name="sum_z",
    )(sums, scale)


def solution(mesh):
    vocab, width = mesh.devices.shape
    sizes = (4, vocab // 8, 2)
    inner = Mesh(mesh.devices.reshape(*sizes, width), ("y", "z", "c", "w"))
    vocab_axes = ("y", "z", "c")
    placed = (P(None, "w"), P(vocab_axes, "w"), P(), P())
    return jax.shard_map(
        functools.partial(on_device, sizes),
        mesh=inner,
        in_specs=placed,
        out_specs=P(vocab_axes, "w"),
        check_vma=False,
    )
```

```python
import functools
import jax
import jax.numpy as jnp
from jax import lax
from jax.experimental import pallas as pl
from jax.experimental.pallas import tpu as pltpu
from jax.sharding import Mesh, PartitionSpec as P

logit_cap = 30.0
zloss_weight = 0.001

f32, bf16, i16, i32 = jnp.float32, jnp.bfloat16, jnp.int16, jnp.int32

SIDE = 16
LANES = 128
TOP = 32767.0
VMEM_BYTES = 18 * 1024 * 1024


def exponent_of(largest):
    return jnp.floor(jnp.log2(jnp.maximum(largest, 1e-30))) - 14.0


def code(values, exponent):
    scaled = jnp.floor(values * jnp.exp2(-exponent) + 0.5)
    return jnp.clip(scaled, -TOP, TOP).astype(i32).astype(i16)


def to_f32(codes):
    return codes.astype(i32).astype(f32)


def token_order(sizes, tokens):
    ny, nz, nc = sizes
    pair = tokens // (ny * nz * nc)
    place = lax.broadcasted_iota(i32, (tokens, tokens), 0)
    token = lax.broadcasted_iota(i32, (tokens, tokens), 1)
    core = place // (ny * nz * pair)
    yz = (place // pair) % (ny * nz)
    r = place % pair
    return token == (yz * nc + core) * pair + r


def column_of(mask, row):
    return jnp.sum(jnp.where(mask, row, 0.0), axis=1, keepdims=True)


def eye(n):
    return lax.broadcasted_iota(i32, (n, n), 0) == lax.broadcasted_iota(i32, (n, n), 1)


def rows_of(part, columns):
    return pl.ds(pl.multiple_of(part * columns, columns), columns)


def store_coded(partial, out_ref):
    tokens = partial.shape[0]
    exponent = exponent_of(jnp.max(jnp.abs(partial), axis=0, keepdims=True))
    out_ref[0:tokens, :] = code(partial, exponent)
    out_ref[tokens:, :] = jnp.broadcast_to(
        exponent, (SIDE, exponent.shape[1])
    ).astype(i32).astype(i16)


def logits_kernel(
    sizes, hidden_hbm, weight_hbm, targets_hbm, scale_hbm,
    out_ref, place_ref, own_scale_ref, hard_ref, weight_ref,
    hidden_ref, part_ref, targets_ref, scale_ref, sems, weight_sems,
):
    tokens = hidden_ref.shape[0]
    pair = own_scale_ref.shape[0]
    parts, _, columns = out_ref.shape
    sources = [(hidden_hbm, hidden_ref), (targets_hbm, targets_ref), (scale_hbm, scale_ref)]
    for part in range(parts):
        sources.append((weight_hbm.at[pl.ds(part * columns, columns)], part_ref.at[part]))
    copies = [
        pltpu.make_async_copy(source, target, sems.at[at])
        for at, (source, target) in enumerate(sources)
    ]
    for copy in copies:
        copy.start()
    ordering = token_order(sizes, tokens)
    order = jnp.where(ordering, 1.0, 0.0).astype(bf16)
    ny, nz, nc = sizes
    device = (lax.axis_index("y") * nz + lax.axis_index("z")) * nc + lax.axis_index("c")
    copies[0].wait()
    ordered = jnp.dot(order, hidden_ref[...], preferred_element_type=f32).astype(bf16)
    for copy in copies[1:3]:
        copy.wait()
    place = column_of(ordering, (targets_ref[...] - device * (parts * columns)).astype(f32))
    place_ref[...] = jnp.broadcast_to(place, place_ref.shape)
    mine = lax.broadcasted_iota(i32, (pair, tokens), 1) == (
        device * pair + lax.broadcasted_iota(i32, (pair, tokens), 0)
    )
    own_scale_ref[...] = jnp.broadcast_to(column_of(mine, scale_ref[...]), own_scale_ref.shape)
    last = None
    for part in range(parts):
        copies[3 + part].wait()
        partial = lax.dot_general(
            ordered, part_ref[part], (((1,), (1,)), ((), ())), preferred_element_type=f32
        )
        if last is not None:
            store_coded(last, out_ref.at[part - 1])
        last = partial
    store_coded(last, out_ref.at[parts - 1])

    @pl.when(lax.axis_index("c") == 0)
    def _():
        target_rows(weight_hbm, place_ref, hard_ref, weight_ref, weight_sems)


def exp_kernel(codes_ref, place_ref, out_ref):
    parts, rows, columns = codes_ref.shape
    tokens = rows - SIDE
    raw = None
    for part in range(parts):
        exponent = to_f32(codes_ref[part, tokens:, :])[0:1]
        term = to_f32(codes_ref[part, 0:tokens, :]) * jnp.exp2(exponent)
        raw = term if raw is None else raw + term
    tangent = jnp.tanh(raw / logit_cap)
    exp_terms = jnp.exp(logit_cap * tangent)
    slope = 1.0 - tangent * tangent
    sums = jnp.sum(exp_terms, axis=1, keepdims=True)
    targets = place_ref[:, 0:1]
    places = lax.broadcasted_iota(i32, raw.shape, 1) + lax.axis_index("w") * columns
    at_target = jnp.sum(
        jnp.where(targets == places.astype(f32), slope, 0.0), axis=1, keepdims=True
    )
    diagonal = eye(tokens)
    sum_row = jnp.sum(jnp.where(diagonal, sums, 0.0), axis=0, keepdims=True)
    target_row = jnp.sum(jnp.where(diagonal, at_target, 0.0), axis=0, keepdims=True)
    which = lax.broadcasted_iota(i32, (SIDE, tokens), 0)
    side = jnp.where(which == 0, sum_row, jnp.where(which == 1, target_row, 0.0))
    high = side.astype(bf16)
    low = (side - high.astype(f32)).astype(bf16)
    pieces = [high, low]
    if columns > 2 * tokens:
        pieces.append(jnp.zeros((SIDE, columns - 2 * tokens), bf16))
    grads = (exp_terms * slope).astype(bf16)
    side = jnp.concatenate(pieces, axis=1)
    for part in range(out_ref.shape[0]):
        out_ref[part, 0:tokens, :] = grads
        out_ref[part, tokens:, :] = side


def target_rows(weight_hbm, place_ref, rows_ref, weight_ref, sems):
    tokens = rows_ref.shape[0]
    blocks = sems.shape[0]
    columns = weight_ref.shape[0] // blocks
    copies = []
    for at in range(blocks):
        block = pl.ds(at * columns, columns)
        copies.append(
            pltpu.make_async_copy(weight_hbm.at[block], weight_ref.at[block], sems.at[at])
        )
        copies[-1].start()
    targets = place_ref[:, 0:1]
    lane = lax.broadcasted_iota(i32, (tokens, columns), 1)
    total = None
    for at in range(blocks):
        at_target = targets == (lane + at * columns).astype(f32)
        at_target = jnp.where(at_target, 1.0, 0.0).astype(bf16)
        copies[at].wait()
        weight = weight_ref[pl.ds(at * columns, columns)]
        term = jnp.dot(at_target, weight, preferred_element_type=f32)
        total = term if total is None else total + term
    rows_ref[...] = total.astype(bf16)


def hidden_rows(which, own, grads_ref, weight_ref, hard_ref):
    parts, rows, columns = grads_ref.shape
    tokens = rows - SIDE
    mine = pl.ds(which * own, own)
    side = None
    for part in range(parts):
        term = grads_ref[part, tokens:, :].astype(f32)
        term = term[:, 0:tokens] + term[:, tokens : 2 * tokens]
        side = term if side is None else side + term
    token = lax.broadcasted_iota(i32, (own, tokens), 1)
    mask = token == lax.broadcasted_iota(i32, (own, tokens), 0) + which * own
    sums = column_of(mask, side[0:1, :])
    slope = column_of(mask, side[1:2, :])
    soft = None
    for part in range(parts):
        weight = weight_ref[pl.ds(part * columns, columns)]
        term = jnp.dot(grads_ref[part, mine, :], weight, preferred_element_type=f32)
        soft = term if soft is None else soft + term
    return soft, hard_ref[mine].astype(f32) * slope, sums


def other_hidden_kernel(
    grads_ref, weight_hbm, place_ref, hard_ref, weight_ref,
    other_ref, late_hard_ref, late_weight_ref, sems,
):
    own = other_ref.shape[1]

    @pl.when(lax.axis_index("c") == 0)
    def _():
        store_rows(other_ref, *hidden_rows(1, own, grads_ref, weight_ref, hard_ref))

    @pl.when(lax.axis_index("c") == 1)
    def _():
        target_rows(weight_hbm, place_ref, late_hard_ref, late_weight_ref, sems)
        store_rows(other_ref, *hidden_rows(0, own, grads_ref, late_weight_ref, late_hard_ref))


def own_hidden_kernel(
    grads_ref, hard_ref, weight_ref, late_hard_ref, late_weight_ref, out_ref
):
    own = out_ref.shape[0]
    width = weight_ref.shape[1]

    def store(soft, hard, sums):
        out_ref[:, 0:width] = soft
        out_ref[:, width : 2 * width] = hard
        out_ref[:, 2 * width :] = jnp.broadcast_to(sums, (own, LANES))

    @pl.when(lax.axis_index("c") == 0)
    def _():
        store(*hidden_rows(0, own, grads_ref, weight_ref, hard_ref))

    @pl.when(lax.axis_index("c") == 1)
    def _():
        store(*hidden_rows(1, own, grads_ref, late_weight_ref, late_hard_ref))


def scalar_codes(values):
    exponent = jnp.floor(jnp.log2(jnp.maximum(values, 1e-30))) - 24.0
    scaled = values * jnp.exp2(-exponent)
    high = jnp.floor(scaled * (1.0 / 4096.0))
    return [exponent, high, scaled - high * 4096.0]


def scalar_of(side, at):
    return (side[:, at + 1 : at + 2] * 4096.0 + side[:, at + 2 : at + 3]) * jnp.exp2(
        side[:, at : at + 1]
    )


def in_lanes(columns):
    lane = lax.broadcasted_iota(i32, (columns[0].shape[0], LANES), 1)
    side = jnp.zeros(lane.shape, f32)
    for at, value in enumerate(columns):
        side = jnp.where(lane == at, value, side)
    return side.astype(i32).astype(i16)


def row_exponent(values):
    return exponent_of(jnp.max(jnp.abs(values), axis=1, keepdims=True))


def store_rows(out_ref, soft, hard, total):
    soft_exp, hard_exp = row_exponent(soft), row_exponent(hard)
    pieces = (
        code(soft, soft_exp),
        code(hard, hard_exp),
        in_lanes([soft_exp, hard_exp, *scalar_codes(total)]),
    )
    parts, rows, _ = out_ref.shape
    at = 0
    for piece in pieces:
        for part in range(parts):
            out_ref[part, :, at : at + piece.shape[1]] = piece[part * rows : (part + 1) * rows]
        at += piece.shape[1]


def decoded_sum(width, in_ref):
    sums = None
    for part in range(in_ref.shape[0]):
        side = to_f32(in_ref[part, :, 2 * width :])
        terms = (
            to_f32(in_ref[part, :, 0:width]) * jnp.exp2(side[:, 0:1]),
            to_f32(in_ref[part, :, width : 2 * width]) * jnp.exp2(side[:, 1:2]),
            scalar_of(side, 2),
        )
        sums = terms if sums is None else tuple(a + b for a, b in zip(sums, terms))
    return sums


def cores_kernel(width, mine_ref, other_ref, out_ref):
    soft, hard, total = decoded_sum(width, other_ref)
    soft = soft + mine_ref[:, 0:width]
    hard = hard + mine_ref[:, width : 2 * width]
    store_rows(out_ref, soft, hard, total + mine_ref[:, 2 * width : 2 * width + 1])


def y_kernel(width, in_ref, out_ref):
    store_rows(out_ref, *decoded_sum(width, in_ref))


def z_kernel(width, in_ref, scale_ref, out_ref):
    soft, hard, total = decoded_sum(width, in_ref)
    scale = scale_ref[:, 0:1]
    weighting = scale * (1.0 + 2.0 * zloss_weight * jnp.log(total))
    out_ref[...] = (weighting / total * soft - scale * hard).astype(bf16)


def params():
    return pltpu.CompilerParams(vmem_limit_bytes=VMEM_BYTES)


def on_device(sizes, hidden, head_weight, targets, token_scale):
    ny, nz, nc = sizes
    nw = lax.axis_size("w")
    tokens, width = hidden.shape
    vocab = head_weight.shape[0]
    columns = vocab // nw
    rows = tokens + SIDE
    pair = tokens // (ny * nz * nc)
    lanes = 2 * width + LANES
    hbm = pl.BlockSpec(memory_space=pltpu.HBM)
    vmem = pl.BlockSpec(memory_space=pltpu.VMEM)

    def shape(*dims, dtype=f32):
        return jax.ShapeDtypeStruct(dims, dtype)

    def swap(x):
        return lax.ppermute(x, "c", [(0, 1), (1, 0)])

    in_hbm = functools.partial(pltpu.with_memory_space_constraint, memory_space=pltpu.HBM)
    weight_hbm = in_hbm(head_weight)
    hard_shapes = [shape(tokens, width, dtype=bf16), shape(vocab, width, dtype=bf16)]
    codes, place, scale, *hard = pl.pallas_call(
        functools.partial(logits_kernel, sizes),
        in_specs=[hbm] * 4,
        out_specs=[vmem] * 5,
        out_shape=[
            shape(nw, rows, columns, dtype=i16),
            shape(tokens, LANES),
            shape(pair, LANES),
            *hard_shapes,
        ],
        scratch_shapes=[
            pltpu.VMEM((tokens, width), bf16),
            pltpu.VMEM((nw, columns, width), bf16),
            pltpu.VMEM((1, tokens), i32),
            pltpu.VMEM((1, tokens), f32),
            pltpu.SemaphoreType.DMA((nw + 3,)),
            pltpu.SemaphoreType.DMA((nw,)),
        ],
        compiler_params=params(),
        name="logits",
    )(
        in_hbm(hidden),
        weight_hbm,
        in_hbm(targets.reshape(1, tokens)),
        in_hbm(token_scale.reshape(1, tokens)),
    )
    codes = lax.all_to_all(codes, "w", 0, 0, tiled=True)
    grads = pl.pallas_call(
        exp_kernel,
        out_shape=shape(nw, rows, columns, dtype=bf16),
        compiler_params=params(),
        name="exponentials",
    )(codes, place)
    grads = lax.all_to_all(grads, "w", 0, 0, tiled=True)
    other, *late_hard = pl.pallas_call(
        other_hidden_kernel,
        in_specs=[vmem, hbm] + [vmem] * 3,
        out_specs=[vmem] * 3,
        out_shape=[shape(1, tokens // nc, lanes, dtype=i16), *hard_shapes],
        scratch_shapes=[pltpu.SemaphoreType.DMA((nw,))],
        compiler_params=params(),
        name="other_hidden",
    )(grads, weight_hbm, place, *hard)
    other = swap(other)
    mine = pl.pallas_call(
        own_hidden_kernel,
        out_shape=shape(tokens // nc, lanes),
        compiler_params=params(),
        name="own_hidden",
    )(grads, *hard, *late_hard)
    sums = pl.pallas_call(
        functools.partial(cores_kernel, width),
        out_shape=shape(ny, nz * pair, lanes, dtype=i16),
        compiler_params=params(),
        name="sum_cores",
    )(mine, other)
    sums = lax.all_to_all(sums, "y", 0, 0, tiled=True)
    sums = pl.pallas_call(
        functools.partial(y_kernel, width),
        out_shape=shape(nz, pair, lanes, dtype=i16),
        compiler_params=params(),
        name="sum_y",
    )(sums)
    sums = lax.all_to_all(sums, "z", 0, 0, tiled=True)
    return pl.pallas_call(
        functools.partial(z_kernel, width),
        out_shape=shape(pair, width, dtype=bf16),
        compiler_params=params(),
        name="sum_z",
    )(sums, scale)


def solution(mesh):
    vocab, width = mesh.devices.shape
    sizes = (4, vocab // 8, 2)
    inner = Mesh(mesh.devices.reshape(*sizes, width), ("y", "z", "c", "w"))
    vocab_axes = ("y", "z", "c")
    placed = (P(None, "w"), P(vocab_axes, "w"), P(), P())
    return jax.shard_map(
        functools.partial(on_device, sizes),
        mesh=inner,
        in_specs=placed,
        out_specs=P(vocab_axes, "w"),
        check_vma=False,
    )
```

```python
import functools
import jax
import jax.numpy as jnp
from jax import lax
from jax.experimental import pallas as pl
from jax.experimental.pallas import tpu as pltpu
from jax.sharding import Mesh, PartitionSpec as P

logit_cap = 30.0
zloss_weight = 0.001

f32, bf16, i16, i32 = jnp.float32, jnp.bfloat16, jnp.int16, jnp.int32

SIDE = 16
LANES = 128
TOP = 32767.0
VMEM_BYTES = 18 * 1024 * 1024


def exponent_of(largest):
    return jnp.floor(jnp.log2(jnp.maximum(largest, 1e-30))) - 14.0


def code(values, exponent):
    scaled = jnp.floor(values * jnp.exp2(-exponent) + 0.5)
    return jnp.clip(scaled, -TOP, TOP).astype(i32).astype(i16)


def to_f32(codes):
    return codes.astype(i32).astype(f32)


def token_order(sizes, tokens):
    ny, nz, nc = sizes
    pair = tokens // (ny * nz * nc)
    place = lax.broadcasted_iota(i32, (tokens, tokens), 0)
    token = lax.broadcasted_iota(i32, (tokens, tokens), 1)
    core = place // (ny * nz * pair)
    yz = (place // pair) % (ny * nz)
    r = place % pair
    return token == (yz * nc + core) * pair + r


def column_of(mask, row):
    return jnp.sum(jnp.where(mask, row, 0.0), axis=1, keepdims=True)


def eye(n):
    return lax.broadcasted_iota(i32, (n, n), 0) == lax.broadcasted_iota(i32, (n, n), 1)


def rows_of(part, columns):
    return pl.ds(pl.multiple_of(part * columns, columns), columns)


def store_coded(partial, out_ref):
    tokens = partial.shape[0]
    exponent = exponent_of(jnp.max(jnp.abs(partial), axis=0, keepdims=True))
    out_ref[0:tokens, :] = code(partial, exponent)
    out_ref[tokens:, :] = jnp.broadcast_to(
        exponent, (SIDE, exponent.shape[1])
    ).astype(i32).astype(i16)


def logits_kernel(
    sizes, hidden_hbm, weight_hbm, targets_hbm, scale_hbm,
    out_ref, place_ref, own_scale_ref, hard_ref, weight_ref,
    hidden_ref, part_ref, targets_ref, scale_ref, sems, weight_sems,
):
    tokens = hidden_ref.shape[0]
    pair = own_scale_ref.shape[0]
    parts, _, columns = out_ref.shape
    sources = [(hidden_hbm, hidden_ref), (targets_hbm, targets_ref), (scale_hbm, scale_ref)]
    for part in range(parts):
        sources.append((weight_hbm.at[pl.ds(part * columns, columns)], part_ref.at[part]))
    copies = [
        pltpu.make_async_copy(source, target, sems.at[at])
        for at, (source, target) in enumerate(sources)
    ]
    for copy in copies:
        copy.start()
    ordering = token_order(sizes, tokens)
    order = jnp.where(ordering, 1.0, 0.0).astype(bf16)
    ny, nz, nc = sizes
    device = (lax.axis_index("y") * nz + lax.axis_index("z")) * nc + lax.axis_index("c")
    copies[0].wait()
    ordered = jnp.dot(order, hidden_ref[...], preferred_element_type=f32).astype(bf16)
    for copy in copies[1:3]:
        copy.wait()
    place = column_of(ordering, (targets_ref[...] - device * (parts * columns)).astype(f32))
    place_ref[...] = jnp.broadcast_to(place, place_ref.shape)
    mine = lax.broadcasted_iota(i32, (pair, tokens), 1) == (
        device * pair + lax.broadcasted_iota(i32, (pair, tokens), 0)
    )
    own_scale_ref[...] = jnp.broadcast_to(column_of(mine, scale_ref[...]), own_scale_ref.shape)
    last = None
    for part in range(parts):
        copies[3 + part].wait()
        partial = lax.dot_general(
            ordered, part_ref[part], (((1,), (1,)), ((), ())), preferred_element_type=f32
        )
        if last is not None:
            store_coded(last, out_ref.at[part - 1])
        last = partial
    store_coded(last, out_ref.at[parts - 1])

    @pl.when(lax.axis_index("c") == 0)
    def _():
        target_rows(weight_hbm, place_ref, hard_ref, weight_ref, weight_sems)


def exp_kernel(codes_ref, place_ref, out_ref):
    parts, rows, columns = codes_ref.shape
    tokens = rows - SIDE
    raw = None
    for part in range(parts):
        exponent = to_f32(codes_ref[part, tokens:, :])[0:1]
        term = to_f32(codes_ref[part, 0:tokens, :]) * jnp.exp2(exponent)
        raw = term if raw is None else raw + term
    tangent = jnp.tanh(raw / logit_cap)
    exp_terms = jnp.exp(logit_cap * tangent)
    slope = 1.0 - tangent * tangent
    sums = jnp.sum(exp_terms, axis=1, keepdims=True)
    targets = place_ref[:, 0:1]
    places = lax.broadcasted_iota(i32, raw.shape, 1) + lax.axis_index("w") * columns
    at_target = jnp.sum(
        jnp.where(targets == places.astype(f32), slope, 0.0), axis=1, keepdims=True
    )
    diagonal = eye(tokens)
    sum_row = jnp.sum(jnp.where(diagonal, sums, 0.0), axis=0, keepdims=True)
    target_row = jnp.sum(jnp.where(diagonal, at_target, 0.0), axis=0, keepdims=True)
    which = lax.broadcasted_iota(i32, (SIDE, tokens), 0)
    side = jnp.where(which == 0, sum_row, jnp.where(which == 1, target_row, 0.0))
    high = side.astype(bf16)
    low = (side - high.astype(f32)).astype(bf16)
    pieces = [high, low]
    if columns > 2 * tokens:
        pieces.append(jnp.zeros((SIDE, columns - 2 * tokens), bf16))
    grads = (exp_terms * slope).astype(bf16)
    side = jnp.concatenate(pieces, axis=1)
    for part in range(out_ref.shape[0]):
        out_ref[part, 0:tokens, :] = grads
        out_ref[part, tokens:, :] = side


def target_rows(weight_hbm, place_ref, rows_ref, weight_ref, sems):
    tokens = rows_ref.shape[0]
    blocks = sems.shape[0]
    columns = weight_ref.shape[0] // blocks
    copies = []
    for at in range(blocks):
        block = pl.ds(at * columns, columns)
        copies.append(
            pltpu.make_async_copy(weight_hbm.at[block], weight_ref.at[block], sems.at[at])
        )
        copies[-1].start()
    targets = place_ref[:, 0:1]
    lane = lax.broadcasted_iota(i32, (tokens, columns), 1)
    total = None
    for at in range(blocks):
        at_target = targets == (lane + at * columns).astype(f32)
        at_target = jnp.where(at_target, 1.0, 0.0).astype(bf16)
        copies[at].wait()
        weight = weight_ref[pl.ds(at * columns, columns)]
        term = jnp.dot(at_target, weight, preferred_element_type=f32)
        total = term if total is None else total + term
    rows_ref[...] = total.astype(bf16)


def hidden_rows(which, own, grads_ref, weight_ref, hard_ref):
    parts, rows, columns = grads_ref.shape
    tokens = rows - SIDE
    mine = pl.ds(which * own, own)
    side = None
    for part in range(parts):
        term = grads_ref[part, tokens:, :].astype(f32)
        term = term[:, 0:tokens] + term[:, tokens : 2 * tokens]
        side = term if side is None else side + term
    token = lax.broadcasted_iota(i32, (own, tokens), 1)
    mask = token == lax.broadcasted_iota(i32, (own, tokens), 0) + which * own
    sums = column_of(mask, side[0:1, :])
    slope = column_of(mask, side[1:2, :])
    soft = None
    for part in range(parts):
        weight = weight_ref[pl.ds(part * columns, columns)]
        term = jnp.dot(grads_ref[part, mine, :], weight, preferred_element_type=f32)
        soft = term if soft is None else soft + term
    return soft, hard_ref[mine].astype(f32) * slope, sums


def other_hidden_kernel(
    grads_ref, weight_hbm, place_ref, hard_ref, weight_ref,
    other_ref, late_hard_ref, late_weight_ref, sems,
):
    own = other_ref.shape[1]

    @pl.when(lax.axis_index("c") == 0)
    def _():
        store_rows(other_ref, *hidden_rows(1, own, grads_ref, weight_ref, hard_ref))

    @pl.when(lax.axis_index("c") == 1)
    def _():
        target_rows(weight_hbm, place_ref, late_hard_ref, late_weight_ref, sems)
        store_rows(other_ref, *hidden_rows(0, own, grads_ref, late_weight_ref, late_hard_ref))


def own_hidden_kernel(
    grads_ref, hard_ref, weight_ref, late_hard_ref, late_weight_ref, out_ref
):
    own = out_ref.shape[0]
    width = weight_ref.shape[1]

    def store(soft, hard, sums):
        out_ref[:, 0:width] = soft
        out_ref[:, width : 2 * width] = hard
        out_ref[:, 2 * width :] = jnp.broadcast_to(sums, (own, LANES))

    @pl.when(lax.axis_index("c") == 0)
    def _():
        store(*hidden_rows(0, own, grads_ref, weight_ref, hard_ref))

    @pl.when(lax.axis_index("c") == 1)
    def _():
        store(*hidden_rows(1, own, grads_ref, late_weight_ref, late_hard_ref))


def scalar_codes(values):
    exponent = jnp.floor(jnp.log2(jnp.maximum(values, 1e-30))) - 24.0
    scaled = values * jnp.exp2(-exponent)
    high = jnp.floor(scaled * (1.0 / 4096.0))
    return [exponent, high, scaled - high * 4096.0]


def scalar_of(side, at):
    return (side[:, at + 1 : at + 2] * 4096.0 + side[:, at + 2 : at + 3]) * jnp.exp2(
        side[:, at : at + 1]
    )


def in_lanes(columns):
    lane = lax.broadcasted_iota(i32, (columns[0].shape[0], LANES), 1)
    side = jnp.zeros(lane.shape, f32)
    for at, value in enumerate(columns):
        side = jnp.where(lane == at, value, side)
    return side.astype(i32).astype(i16)


def row_exponent(values):
    return exponent_of(jnp.max(jnp.abs(values), axis=1, keepdims=True))


def store_rows(out_ref, soft, hard, total):
    soft_exp, hard_exp = row_exponent(soft), row_exponent(hard)
    pieces = (
        code(soft, soft_exp),
        code(hard, hard_exp),
        in_lanes([soft_exp, hard_exp, *scalar_codes(total)]),
    )
    parts, rows, _ = out_ref.shape
    at = 0
    for piece in pieces:
        for part in range(parts):
            out_ref[part, :, at : at + piece.shape[1]] = piece[part * rows : (part + 1) * rows]
        at += piece.shape[1]


def decoded_sum(width, in_ref):
    sums = None
    for part in range(in_ref.shape[0]):
        side = to_f32(in_ref[part, :, 2 * width :])
        terms = (
            to_f32(in_ref[part, :, 0:width]) * jnp.exp2(side[:, 0:1]),
            to_f32(in_ref[part, :, width : 2 * width]) * jnp.exp2(side[:, 1:2]),
            scalar_of(side, 2),
        )
        sums = terms if sums is None else tuple(a + b for a, b in zip(sums, terms))
    return sums


def cores_kernel(width, mine_ref, other_ref, out_ref):
    soft, hard, total = decoded_sum(width, other_ref)
    soft = soft + mine_ref[:, 0:width]
    hard = hard + mine_ref[:, width : 2 * width]
    store_rows(out_ref, soft, hard, total + mine_ref[:, 2 * width : 2 * width + 1])


def y_kernel(width, in_ref, out_ref):
    store_rows(out_ref, *decoded_sum(width, in_ref))


def z_kernel(width, in_ref, scale_ref, out_ref):
    rows, pair = in_ref.shape[0], out_ref.shape[0]
    side = to_f32(in_ref[:, 2 * width :])
    sums = (
        to_f32(in_ref[:, 0:width]) * jnp.exp2(side[:, 0:1]),
        to_f32(in_ref[:, width : 2 * width]) * jnp.exp2(side[:, 1:2]),
        scalar_of(side, 2),
    )
    while rows > pair:
        rows //= 2
        sums = tuple(x[0:rows] + x[rows:] for x in sums)
    soft, hard, total = sums
    scale = scale_ref[:, 0:1]
    weighting = scale * (1.0 + 2.0 * zloss_weight * jnp.log(total))
    out_ref[...] = (weighting / total * soft - scale * hard).astype(bf16)


def params():
    return pltpu.CompilerParams(vmem_limit_bytes=VMEM_BYTES)


def on_device(sizes, hidden, head_weight, targets, token_scale):
    ny, nz, nc = sizes
    nw = lax.axis_size("w")
    tokens, width = hidden.shape
    vocab = head_weight.shape[0]
    columns = vocab // nw
    rows = tokens + SIDE
    pair = tokens // (ny * nz * nc)
    lanes = 2 * width + LANES
    hbm = pl.BlockSpec(memory_space=pltpu.HBM)
    vmem = pl.BlockSpec(memory_space=pltpu.VMEM)

    def shape(*dims, dtype=f32):
        return jax.ShapeDtypeStruct(dims, dtype)

    def swap(x):
        return lax.ppermute(x, "c", [(0, 1), (1, 0)])

    in_hbm = functools.partial(pltpu.with_memory_space_constraint, memory_space=pltpu.HBM)
    weight_hbm = in_hbm(head_weight)
    hard_shapes = [shape(tokens, width, dtype=bf16), shape(vocab, width, dtype=bf16)]
    codes, place, scale, *hard = pl.pallas_call(
        functools.partial(logits_kernel, sizes),
        in_specs=[hbm] * 4,
        out_specs=[vmem] * 5,
        out_shape=[
            shape(nw, rows, columns, dtype=i16),
            shape(tokens, LANES),
            shape(pair, LANES),
            *hard_shapes,
        ],
        scratch_shapes=[
            pltpu.VMEM((tokens, width), bf16),
            pltpu.VMEM((nw, columns, width), bf16),
            pltpu.VMEM((1, tokens), i32),
            pltpu.VMEM((1, tokens), f32),
            pltpu.SemaphoreType.DMA((nw + 3,)),
            pltpu.SemaphoreType.DMA((nw,)),
        ],
        compiler_params=params(),
        name="logits",
    )(
        in_hbm(hidden),
        weight_hbm,
        in_hbm(targets.reshape(1, tokens)),
        in_hbm(token_scale.reshape(1, tokens)),
    )
    codes = lax.all_to_all(codes, "w", 0, 0, tiled=True)
    grads = pl.pallas_call(
        exp_kernel,
        out_shape=shape(nw, rows, columns, dtype=bf16),
        compiler_params=params(),
        name="exponentials",
    )(codes, place)
    grads = lax.all_to_all(grads, "w", 0, 0, tiled=True)
    other, *late_hard = pl.pallas_call(
        other_hidden_kernel,
        in_specs=[vmem, hbm] + [vmem] * 3,
        out_specs=[vmem] * 3,
        out_shape=[shape(1, tokens // nc, lanes, dtype=i16), *hard_shapes],
        scratch_shapes=[pltpu.SemaphoreType.DMA((nw,))],
        compiler_params=params(),
        name="other_hidden",
    )(grads, weight_hbm, place, *hard)
    other = swap(other)
    mine = pl.pallas_call(
        own_hidden_kernel,
        out_shape=shape(tokens // nc, lanes),
        compiler_params=params(),
        name="own_hidden",
    )(grads, *hard, *late_hard)
    sums = pl.pallas_call(
        functools.partial(cores_kernel, width),
        out_shape=shape(ny, nz * pair, lanes, dtype=i16),
        compiler_params=params(),
        name="sum_cores",
    )(mine, other)
    sums = lax.all_to_all(sums, "y", 0, 0, tiled=True)
    sums = pl.pallas_call(
        functools.partial(y_kernel, width),
        out_shape=shape(nz, pair, lanes, dtype=i16),
        compiler_params=params(),
        name="sum_y",
    )(sums)
    sums = lax.all_to_all(sums, "z", 0, 0, tiled=True)
    return pl.pallas_call(
        functools.partial(z_kernel, width),
        out_shape=shape(pair, width, dtype=bf16),
        compiler_params=params(),
        name="sum_z",
    )(sums.reshape(nz * pair, lanes), scale)


def solution(mesh):
    vocab, width = mesh.devices.shape
    sizes = (4, vocab // 8, 2)
    inner = Mesh(mesh.devices.reshape(*sizes, width), ("y", "z", "c", "w"))
    vocab_axes = ("y", "z", "c")
    placed = (P(None, "w"), P(vocab_axes, "w"), P(), P())
    return jax.shard_map(
        functools.partial(on_device, sizes),
        mesh=inner,
        in_specs=placed,
        out_specs=P(vocab_axes, "w"),
        check_vma=False,
    )
```
